32 devices in a mesh: groups: 2 (over x), fsdp: 16 (over z, y, core).
Axes of the slice: x: 2, y: 2, z: 4, core: 2. Of those that a mesh axis runs over, the one named last changes fastest.
Arguments:
- activations: bfloat16 [4096, 8192], P(('groups', 'fsdp')), parts along dimension 0, may hold values from -6 to 6
- grad_out: bfloat16 [4096, 1024], P(('groups', 'fsdp')), parts along dimension 0, may hold values from -6 to 6
- base_weight: bfloat16 [8192, 1024], P('fsdp'), may hold values from -0.1875 to 0.1875
- adapter_down: bfloat16 [16, 8192, 128], P('fsdp'), may hold values from -0.5 to 0.5
- adapter_up: bfloat16 [16, 128, 1024], P('fsdp'), may hold values from -0.5 to 0.5
- row_tenant: int32 [4096, 1], P(('groups', 'fsdp')), parts along dimension 0, may hold values from 0 to 15; in each aligned block of 128 rows (0 to 127, 128 to 255, ...) at most 16 rows name the same one
- rank_bucket: int32 [16], replicated, may hold values from 0 to 2
- owner_slot: int32 [16], replicated, may hold values from 0 to 15, each once
Outputs:
- input_gradient: bfloat16 [4096, 8192], P(('groups', 'fsdp')), parts along dimension 0
- grad_down: float32 [32, 8192, 128], P(('groups', 'fsdp')), parts along dimension 0
- grad_up: float32 [32, 128, 1024], P(('groups', 'fsdp')), parts along dimension 0
The draws below stay inside these ranges and needn't reach their ends.
There are 2 independent parts, one for each index of `groups`. The reference program is written for one: setup_inputs(seed, part) draws one part's arguments, and reference() takes and returns one part's arrays. A program takes and returns all parts, laid end to end along the dimension named above; an argument that names none is the same for every part. Nothing has to cross between parts.
Inputs may be any that keep to these rules, and one draw needn't show every extreme that they name: `row_tenant`: on the rows of one device at most 16 rows belong to one tenant, and some tenant has exactly 16 there; every tenant has rows somewhere. `rank_bucket`: 0, 1 and 2 stand for ranks 8, 32 and 128. `owner_slot`: A permutation of the slots.
All inputs are finite; a program needn't handle non-finite values.
Results may differ from the reference program's by a relative error of at most 0.008.
Values may be sent and summed in bfloat16 or wider, within the bound.
A program may use at most 128 MiB of HBM per device.

```python
import math
import jax
import jax.numpy as jnp
import numpy as np
from jax import lax

MODEL_WIDTH = 8192
KV = 1024
TOK_DEV = 128
R_SMALL = 8
R_MID = 32
RMAX = 128
TOKEN_COUNT = 2048
TENANT_COUNT = 16
CAP = 16
N_FSDP = 16


def with_ends(result, stream_key, least, top_value):
    longest = result.shape.index(max(result.shape))
    spots = []
    for shift in (0, 1):
        where = [jax.random.randint(jax.random.fold_in(stream_key, axis), (), 0, length) for axis, length in enumerate(result.shape)]
        where[longest] = (where[longest] + shift) % result.shape[longest]
        spots.append(tuple(where))
    return result.at[spots[0]].set(least).at[spots[1]].set(top_value)


def levels(key, shape, cuts, least, high):
    level = 1.0
    for position, shards_of in cuts:
        heights = jax.random.uniform(jax.random.fold_in(jax.random.fold_in(key, 6), position), (shards_of,), jnp.float32, least / len(cuts), high / len(cuts))
        level = level * jnp.repeat(jnp.exp(heights), shape[position] // shards_of).reshape((-1,) + (1,) * (len(shape) - 1 - position))
    return level


def deal_out(key, own, number, rows, count, top, bound, slope):
    order = jax.random.permutation(key, count)
    crowded, usual = shares(count, rows * top, bound, slope, True), shares(count, rows * top, bound, slope, False)
    places = jnp.arange(count)

    def named(tallies, offset_by):
        used = int((tallies > 0).sum())
        fixed = max(1, used // 4)
        moved = fixed + (places - fixed + offset_by * (used - fixed)) % max(1, count - fixed)
        return jnp.zeros((count,), jnp.int32).at[order[jnp.where(places < fixed, places, moved)]].set(jnp.asarray(tallies, jnp.int32))

    tallies = jnp.where(number % 4 == 0, named(crowded, number // 4), named(usual, number - number // 4 - 1))
    mixed = jax.random.permutation(jax.random.fold_in(own, 3), count)
    donor, receiver = mixed[0:count // 2 * 2:2], mixed[1:count // 2 * 2:2]
    room = jnp.minimum(tallies[donor] - 1, bound - tallies[receiver]) // 2
    room = jnp.where((donor == order[0]) | (receiver == order[0]) | (tallies[receiver] == 0), 0, jnp.maximum(room, 0))
    moved = jax.random.randint(jax.random.fold_in(own, 4), (count // 2,), 0, 1 << 20) % (room + 1)
    tallies = tallies.at[donor].add(-moved).at[receiver].add(moved)
    items = jnp.searchsorted(jnp.cumsum(tallies), jnp.arange(rows * top), side="right").astype(jnp.int32)
    table = items.reshape(top, rows).T
    table = table[jax.random.permutation(jax.random.fold_in(own, 1), rows)]
    offset_by = jax.random.randint(jax.random.fold_in(own, 2), (rows, 1), 0, top)
    return jnp.take_along_axis(table, (jnp.arange(top)[None, :] + offset_by) % top, axis=1)


def shares(amount, total, most, lean, full):
    loads = [(1 << 20) // math.isqrt(grade ** lean) + 1 for grade in range(1, amount + 1)]
    largest = most if full else min(most, max(-(-total // amount), total * loads[0] // sum(loads)))
    least = 1 if total - largest >= amount - 1 else 0
    given, rest = [largest] + [least] * (amount - 1), total - largest - least * (amount - 1)
    while rest > 0:
        movable = [i for i in range(1, amount) if given[i] < largest] or [i for i in range(1, amount) if given[i] < most]
        pool, left = sum([loads[i] for i in movable]), rest
        for i in movable:
            extra = min(most - given[i], max(1, left * loads[i] // pool), rest)
            given[i] = given[i] + extra
            rest = rest - extra
    return np.array(given)


def normal_values(own_key, extent, deviation, bound, split=(), held_as=jnp.bfloat16):
    gain = levels(own_key, extent, split, -0.22, 0.18) if split else 1.0
    values = jax.random.normal(own_key, extent, jnp.float32) * deviation * gain
    return jnp.minimum(jnp.maximum(values, -bound), bound).astype(held_as)


def setup_inputs(seed: int = 0, part: int = 0) -> dict:
    key_list = jax.random.split(jax.random.key(seed), 9)
    part_keys = jax.random.split(jax.random.fold_in(key_list[8], part), 9)
    activations = normal_values(part_keys[0], (TOKEN_COUNT, MODEL_WIDTH), 1.0, 6.0, ((0, 16),))
    grad_out = normal_values(part_keys[1], (TOKEN_COUNT, KV), 1.0, 6.0, ((0, 16),))
    base_weight = normal_values(key_list[2], (MODEL_WIDTH, KV), KV ** -0.5, 0.1875, ((0, 16),))
    adapter_down = normal_values(key_list[3], (TENANT_COUNT, MODEL_WIDTH, RMAX), RMAX ** -0.5, 0.5, ((0, 16),))
    adapter_up = normal_values(key_list[4], (TENANT_COUNT, RMAX, KV), RMAX ** -0.5, 0.5, ((0, 16),))
    row_tenant_keys = jax.random.split(jax.random.fold_in(part_keys[5], 1), TOKEN_COUNT // TOK_DEV)
    row_tenant_turns = jax.random.permutation(jax.random.fold_in(part_keys[5], 3), TOKEN_COUNT // TOK_DEV)
    row_tenant = jax.vmap(lambda own, number: deal_out(jax.random.fold_in(part_keys[5], 2), own, number, TOK_DEV, TENANT_COUNT, 1, CAP, 2))(row_tenant_keys, row_tenant_turns).reshape((TOKEN_COUNT, 1))
    rank_bucket = with_ends(jax.random.randint(key_list[6], (TENANT_COUNT,), 0, 3), jax.random.fold_in(key_list[6], 1), 0, 2).astype(jnp.int32)
    owner_slot = jax.random.permutation(key_list[7], TENANT_COUNT).astype(jnp.int32)
    return {"activations": activations, "grad_out": grad_out, "base_weight": base_weight, "adapter_down": adapter_down, "adapter_up": adapter_up, "row_tenant": row_tenant, "rank_bucket": rank_bucket, "owner_slot": owner_slot}


adapter_alpha = 16.0


def reference(activations, grad_out, base_weight, adapter_down, adapter_up, row_tenant, rank_bucket, owner_slot):
    tenant = row_tenant[:, 0].astype(jnp.int32)
    frozen_term = jnp.dot(grad_out, base_weight.T, preferred_element_type=jnp.float32).astype(jnp.bfloat16)
    rank_widths = jnp.where(rank_bucket == 0, R_SMALL, jnp.where(rank_bucket == 1, R_MID, RMAX)).astype(jnp.int32)
    tenant_scales = adapter_alpha / rank_widths.astype(jnp.float32)
    onehot = (tenant[:, None] == jnp.arange(TENANT_COUNT, dtype=jnp.int32)[None, :]).astype(jnp.int32)
    per_device = onehot.reshape(N_FSDP, TOK_DEV, TENANT_COUNT)
    earlier = (jnp.cumsum(per_device, axis=1) - per_device).reshape(TOKEN_COUNT, TENANT_COUNT)
    within = jnp.sum(earlier * onehot, axis=1).astype(jnp.int32)
    slot_position = ((jnp.arange(TOKEN_COUNT, dtype=jnp.int32) // TOK_DEV) * CAP + within).astype(jnp.int32)
    row_index = jnp.full((TENANT_COUNT, N_FSDP * CAP), TOKEN_COUNT, jnp.int32)
    row_index = row_index.at[tenant, slot_position].set(jnp.arange(TOKEN_COUNT, dtype=jnp.int32))
    padded_in = jnp.concatenate([activations, jnp.zeros((1, MODEL_WIDTH), activations.dtype)], 0)
    padded_grad = jnp.concatenate([grad_out, jnp.zeros((1, KV), grad_out.dtype)], 0)
    columns = jnp.arange(RMAX, dtype=jnp.int32)

    def single_tenant(adapter_accum, selected_bucket):
        collected_rows = row_index[selected_bucket]
        incoming_rows = padded_in[collected_rows]
        gradient_rows = padded_grad[collected_rows]
        down_weight = adapter_down[owner_slot[selected_bucket]]
        up_weight = adapter_up[owner_slot[selected_bucket]]
        rank_mask = (columns < rank_widths[selected_bucket]).astype(jnp.float32)
        adapter_scale = tenant_scales[selected_bucket]
        hidden_state = (jnp.dot(incoming_rows, down_weight, preferred_element_type=jnp.float32) * rank_mask).astype(jnp.bfloat16)
        backward_rows = (jnp.dot(gradient_rows, up_weight.T, preferred_element_type=jnp.float32) * rank_mask).astype(jnp.bfloat16)
        adapter_rows = (adapter_scale * jnp.dot(backward_rows, down_weight.T, preferred_element_type=jnp.float32)).astype(jnp.bfloat16)
        down_gradient = adapter_scale * jnp.dot(incoming_rows.T, backward_rows, preferred_element_type=jnp.float32)
        up_gradient = adapter_scale * jnp.dot(hidden_state.T, gradient_rows, preferred_element_type=jnp.float32)
        adapter_accum = adapter_accum.at[collected_rows].set(adapter_rows)
        return adapter_accum, (down_gradient, up_gradient)

    initial_accum = jnp.zeros((TOKEN_COUNT + 1, MODEL_WIDTH), jnp.bfloat16)
    adapter_accum, (down_stacked, up_stacked) = lax.scan(single_tenant, initial_accum, jnp.arange(TENANT_COUNT, dtype=jnp.int32))
    grad_down = jnp.zeros_like(down_stacked).at[owner_slot].set(down_stacked)
    grad_up = jnp.zeros_like(up_stacked).at[owner_slot].set(up_stacked)
    input_gradient = (frozen_term.astype(jnp.float32) + adapter_accum[:TOKEN_COUNT].astype(jnp.float32)).astype(jnp.bfloat16)
    return input_gradient, grad_down, grad_up
```

```python
import jax
import jax.numpy as jnp
from jax import lax
from jax.sharding import PartitionSpec as P

R_SMALL = 8
R_MID = 32
RMAX = 128
ALPHA = 16.0


def dot(a, b, dims, batch=((), ())):
    return lax.dot_general(a, b, (dims, batch), preferred_element_type=jnp.float32)


def on_device(
    activations,
    grad_out,
    base_weight,
    adapter_down,
    adapter_up,
    row_tenant,
    rank_bucket,
    owner_slot,
):
    bf16 = jnp.bfloat16
    rows, width = activations.shape
    kv = grad_out.shape[1]
    tenants = rank_bucket.shape[0]
    n = lax.axis_size("fsdp")
    groups = lax.axis_size("groups")
    me = lax.axis_index("fsdp")
    my_group = lax.axis_index("groups")
    cap = max(2, 2 * rows // tenants)
    cols = width // n
    part = cols // groups
    down, up = adapter_down[0], adapter_up[0]

    my_part = lax.dynamic_index_in_dim(
        down.reshape(n, groups, part, RMAX), my_group, axis=1, keepdims=False
    )
    parts = lax.all_to_all(my_part, "fsdp", split_axis=0, concat_axis=0, tiled=True)
    slices = lax.all_gather(parts, "groups", axis=1, tiled=True)

    grad_all = lax.all_gather(grad_out, "fsdp", axis=0, tiled=True).reshape(n, rows, kv)
    tenant = lax.all_gather(row_tenant[:, 0], "fsdp", axis=0, tiled=True).reshape(n, rows)

    same = tenant[:, :, None] == tenant[:, None, :]
    before = jnp.arange(rows)[None, :, None] > jnp.arange(rows)[None, None, :]
    within = jnp.sum((same & before).astype(jnp.int32), axis=2)
    hot = tenant[:, :, None] == jnp.arange(tenants, dtype=jnp.int32)
    slot = jnp.sum(jnp.where(hot, owner_slot, 0), axis=2)
    place = slot * cap + within
    perm = (
        place[:, None, :] == jnp.arange(tenants * cap, dtype=jnp.int32)[None, :, None]
    ).astype(bf16)
    perm_mine = lax.dynamic_index_in_dim(perm, me, axis=0, keepdims=False)
    pick = lax.dynamic_slice_in_dim(perm, me * cap, cap, axis=1)

    bucket_of_slot = jnp.sum(
        jnp.where(owner_slot[None, :] == jnp.arange(tenants)[:, None], rank_bucket[None, :], 0),
        axis=1,
    )
    ranks = jnp.where(bucket_of_slot == 0, R_SMALL, jnp.where(bucket_of_slot == 1, R_MID, RMAX))
    scales = ALPHA / ranks.astype(jnp.float32)
    my_rank, my_scale = ranks[me], scales[me]
    mask = (jnp.arange(RMAX, dtype=jnp.int32) < my_rank).astype(jnp.float32)

    sent = dot(perm_mine, activations, ((1,), (0,))).astype(bf16)
    came = lax.all_to_all(
        sent.reshape(n, cap, width), "fsdp", split_axis=0, concat_axis=0, tiled=True
    ).reshape(n * cap, width)

    grads = dot(pick, grad_all, ((2,), (1,)), ((0,), (0,))).astype(bf16).reshape(n * cap, kv)
    back = (dot(grads, up, ((1,), (1,))) * mask).astype(bf16)
    backs = lax.all_gather(back, "fsdp", axis=0, tiled=True).reshape(tenants, n * cap, RMAX)

    lora = dot(backs, slices, ((2,), (2,)), ((0,), (0,))) * scales[:, None, None]
    lora = lora.astype(bf16).reshape(tenants, n, cap, cols)
    lora = jnp.transpose(lora, (1, 0, 2, 3)).reshape(n, tenants * cap, cols)
    lora = dot(perm, lora, ((1,), (1,)), ((0,), (0,)))
    base = dot(grad_all.reshape(n * rows, kv), base_weight, ((1,), (1,))).astype(bf16)
    total = (base.reshape(n, rows, cols).astype(jnp.float32) + lora).astype(bf16)
    input_gradient = lax.all_to_all(
        total.reshape(n * rows, cols), "fsdp", split_axis=0, concat_axis=1, tiled=True
    )

    hidden = (dot(came, down, ((1,), (0,))) * mask).astype(bf16)
    grad_down = my_scale * dot(came, back, ((0,), (0,)))
    grad_up = my_scale * dot(hidden, grads, ((0,), (0,)))
    return input_gradient, grad_down[None], grad_up[None]


def solution(mesh):
    rows = P(("groups", "fsdp"), None)
    return jax.shard_map(
        on_device,
        mesh=mesh,
        in_specs=(
            rows,
            rows,
            P("fsdp", None),
            P("fsdp", None, None),
            P("fsdp", None, None),
            rows,
            P(),
            P(),
        ),
        out_specs=(
            rows,
            P(("groups", "fsdp"), None, None),
            P(("groups", "fsdp"), None, None),
        ),
        check_vma=False,
    )
```

```python
import functools

import jax
import jax.numpy as jnp
from jax import lax
from jax.experimental import pallas as pl
from jax.experimental.pallas import tpu as pltpu
from jax.sharding import PartitionSpec as P

R_SMALL = 8
R_MID = 32
RMAX = 128
ALPHA = 16.0


def dot(a, b, dims, batch=((), ())):
    return lax.dot_general(a, b, (dims, batch), preferred_element_type=jnp.float32)


MESH = pl.DeviceIdType.MESH


def exchange_kernel(
    n,
    groups,
    pack_ref,
    sent_ref,
    down_ref,
    up_ref,
    weight_ref,
    mask_ref,
    my_scale_ref,
    scales_ref,
    out_ref,
    grad_down_ref,
    grad_up_ref,
    packs,
    came,
    slices,
    backs,
    grads,
    lora,
    total,
    pack_send,
    pack_recv,
    back_send,
    back_recv,
    down_send,
    down_recv,
    x_send,
    x_recv,
    act_send,
    act_recv,
    out_send,
    out_recv,
    local_sem,
):
    bf16 = jnp.bfloat16
    me = lax.axis_index("fsdp")
    group = lax.axis_index("groups")
    cap, width = sent_ref.shape[1], sent_ref.shape[2]
    rows = pack_ref.shape[0]
    kv = grads.shape[2]
    cols = slices.shape[1]
    part = cols // groups
    w = me % 4
    across = me - w + (w + 2) % 4
    beside = me + 1 - 2 * (w % 2)
    line = n // 4

    def remote(src, dst, send, recv, to, to_group=None):
        return pltpu.make_async_remote_copy(
            src_ref=src,
            dst_ref=dst,
            send_sem=send,
            recv_sem=recv,
            device_id=(group if to_group is None else to_group, to),
            device_id_type=MESH,
        )

    def peer(k):
        return lax.rem(me + k, n)

    def source(k):
        return lax.rem(me + n - k, n)

    def loop(first, last, body):
        lax.fori_loop(first, last, lambda k, c: (body(k), c)[1], 0)

    barrier = pltpu.get_barrier_semaphore()
    loop(1, n, lambda k: pl.semaphore_signal(
        barrier, inc=1, device_id=(group, peer(k)), device_id_type=MESH))
    for d in range(1, groups):
        pl.semaphore_signal(
            barrier, inc=1, device_id=((group + d) % groups, me), device_id_type=MESH)

    packs[me] = pack_ref[...]
    keep = pltpu.make_async_copy(sent_ref.at[me], came.at[me], local_sem)
    keep.start()
    slices[me] = down_ref[pl.ds(pl.multiple_of(me * cols, cols), cols), :]
    pl.semaphore_wait(barrier, n - 1 + groups - 1)

    def gather_start(buf, send, recv):
        own = buf.at[me]
        for k in range(1, line):
            remote(own, own, send.at[k], recv.at[k], peer(4 * k)).start()
        remote(own, own, send.at[line], recv.at[line], across).start()
        remote(own, own, send.at[2 * line], recv.at[2 * line], beside).start()

    def gather_finish(buf, send, recv):
        def copy_b(i, k):
            return remote(buf.at[i], buf.at[i], send.at[line + k], recv.at[line + k], across)

        def copy_c(i, k):
            at = 2 * line + k
            return remote(buf.at[i], buf.at[i], send.at[at], recv.at[at], beside)

        def from_line(origin, k):
            return lax.rem(origin + n - 4 * k, n)

        for k in range(1, line):
            i = source(4 * k)
            remote(buf.at[i], buf.at[i], send.at[k], recv.at[k], peer(4 * k)).wait_recv()
            copy_b(i, k).start()
            copy_c(i, k).start()
        for k in range(line):
            i = from_line(across, k)
            copy_b(i, k).wait_recv()
            copy_c(i, line + k).start()
        other = beside - beside % 4 + (beside % 4 + 2) % 4
        for k in range(line):
            copy_c(from_line(beside, k), k).wait_recv()
        for k in range(line):
            copy_c(from_line(other, k), line + k).wait_recv()

    def gather_sent(buf, send, recv):
        for k in range(1, 4 * line):
            remote(buf.at[me], buf.at[me], send.at[k], recv.at[k], beside).wait_send()

    def down_part(k):
        j = peer(k)
        start = pl.multiple_of(j * cols + group * part, part)
        return remote(
            down_ref.at[pl.ds(start, part), :],
            slices.at[me, pl.ds(pl.multiple_of(group * part, part), part), :],
            down_send.at[k], down_recv.at[k], j)

    def place_of(k, owner):
        return slices.at[source(k), pl.ds(pl.multiple_of(owner * part, part), part), :]

    gather_start(packs, pack_send, pack_recv)
    loop(1, n, lambda k: down_part(k).start())
    gather_finish(packs, pack_send, pack_recv)

    def act(k):
        j = peer(k)
        return remote(sent_ref.at[j], came.at[me], act_send.at[k], act_recv.at[k], j)

    wanted = (
        lax.broadcasted_iota(jnp.int32, (n * cap, cap), 0)
        == lax.broadcasted_iota(jnp.int32, (n * cap, cap), 1) + me * cap
    ).astype(bf16)

    def pick(b):
        chosen = dot(packs[b, :, kv:], wanted, ((1,), (0,))).astype(bf16)
        grads[b] = dot(chosen, packs[b, :, :kv], ((0,), (0,))).astype(bf16)

    loop(0, n, pick)
    back = dot(grads[...].reshape(n * cap, kv), up_ref[...], ((1,), (1,))) * mask_ref[...]
    backs[me] = back.astype(bf16)
    gather_start(backs, back_send, back_recv)

    def relay(k):
        remote(place_of(k, group), place_of(k, group), down_send.at[k], down_recv.at[k],
               peer(k)).wait_recv()
        for d in range(1, groups):
            remote(place_of(k, group), place_of(k, group), x_send.at[d, k], x_recv.at[d, k],
                   me, (group + d) % groups).start()

    loop(1, n, relay)
    gather_finish(backs, back_send, back_recv)
    loop(1, n, lambda k: act(k).start())

    def base(b):
        total[b] = dot(packs[b, :, :kv], weight_ref[...], ((1,), (1,))).astype(bf16)

    loop(0, n, base)

    def relayed(k):
        for d in range(1, groups):
            spot = place_of(k, (group + groups - d) % groups)
            remote(spot, spot, x_send.at[d, k], x_recv.at[d, k], me,
                   (group + d) % groups).wait_recv()

    loop(1, n, relayed)

    def low_rank(t):
        term = dot(backs[t], slices[t], ((1,), (1,))) * scales_ref[t]
        lora[:, t] = term.astype(bf16).reshape(n, cap, cols)

    loop(0, n, low_rank)

    def combine(b):
        term = dot(packs[b, :, kv:], lora[b].reshape(n * cap, cols), ((1,), (0,)))
        total[b] = (total[b].astype(jnp.float32) + term).astype(bf16)

    def columns(i):
        return out_ref.at[:, pl.ds(pl.multiple_of(i * cols, cols), cols)]

    def result(k):
        j = peer(k)
        return remote(total.at[j], columns(me), out_send.at[k], out_recv.at[k], j)

    def combine_and_send(k):
        combine(peer(k))
        result(k).start()

    loop(1, n, combine_and_send)
    combine(me)
    out_ref[:, pl.ds(pl.multiple_of(me * cols, cols), cols)] = total[me]

    def arrived(k):
        spot = came.at[source(k)]
        remote(spot, spot, act_send.at[k], act_recv.at[k], peer(k)).wait_recv()

    loop(1, n, arrived)
    keep.wait()
    my_back = backs[me]
    chunk = 1024
    hidden = jnp.zeros((n * cap, RMAX), jnp.float32)
    for c in range(width // chunk):
        at = pl.ds(c * chunk, chunk)
        held = came[:, :, at].reshape(n * cap, chunk)
        hidden += dot(held, down_ref[at, :], ((1,), (0,)))
        grad_down_ref[at, :] = dot(held, my_back, ((0,), (0,))) * my_scale_ref[...]
    hidden = (hidden * mask_ref[...]).astype(bf16)
    up_scale = my_scale_ref[0:1, 0:1]
    grad_up_ref[...] = (
        dot(hidden, grads[...].reshape(n * cap, kv), ((0,), (0,))) * up_scale
    )

    def received(k):
        spot = columns(source(k))
        remote(total.at[me], spot, out_send.at[k], out_recv.at[k], peer(k)).wait_recv()

    loop(1, n, received)
    gather_sent(packs, pack_send, pack_recv)
    gather_sent(backs, back_send, back_recv)

    def all_sent(k):
        down_part(k).wait_send()
        for d in range(1, groups):
            remote(place_of(k, group), place_of(k, group), x_send.at[d, k], x_recv.at[d, k],
                   me, (group + d) % groups).wait_send()
        act(k).wait_send()
        result(k).wait_send()

    loop(1, n, all_sent)


def one_kernel(
    activations,
    grad_out,
    base_weight,
    adapter_down,
    adapter_up,
    row_tenant,
    rank_bucket,
    owner_slot,
):
    bf16, f32 = jnp.bfloat16, jnp.float32
    rows, width = activations.shape
    kv = grad_out.shape[1]
    tenants = rank_bucket.shape[0]
    n = lax.axis_size("fsdp")
    groups = lax.axis_size("groups")
    me = lax.axis_index("fsdp")
    cap = 2 * rows // tenants
    cols = width // n

    tenant = row_tenant[:, 0]
    same = tenant[:, None] == tenant[None, :]
    before = jnp.arange(rows)[:, None] > jnp.arange(rows)[None, :]
    within = jnp.sum((same & before).astype(jnp.int32), axis=1)
    hot = tenant[:, None] == jnp.arange(tenants, dtype=jnp.int32)
    place = jnp.sum(jnp.where(hot, owner_slot, 0), axis=1) * cap + within
    perm = (place[:, None] == jnp.arange(n * cap, dtype=jnp.int32)[None, :]).astype(bf16)
    bucket_of_slot = jnp.sum(
        jnp.where(owner_slot[None, :] == jnp.arange(tenants)[:, None], rank_bucket[None, :], 0),
        axis=1,
    )
    ranks = jnp.where(bucket_of_slot == 0, R_SMALL, jnp.where(bucket_of_slot == 1, R_MID, RMAX))
    scales = ALPHA / ranks.astype(f32)
    mine = jnp.arange(tenants, dtype=jnp.int32) == me
    my_rank = jnp.sum(jnp.where(mine, ranks, 0))
    my_scale = jnp.sum(jnp.where(mine, scales, 0.0))
    mask = (jnp.arange(RMAX, dtype=jnp.int32) < my_rank).astype(f32)[None, :]
    sent = dot(perm, activations, ((0,), (0,))).astype(bf16).reshape(n, cap, width)
    pack = jnp.concatenate([grad_out, perm], axis=1)

    vmem = pl.BlockSpec(memory_space=pltpu.VMEM)
    dma = pltpu.SemaphoreType.DMA
    out, grad_down, grad_up = pl.pallas_call(
        functools.partial(exchange_kernel, n, groups),
        out_shape=(
            jax.ShapeDtypeStruct((rows, width), bf16),
            jax.ShapeDtypeStruct((width, RMAX), f32),
            jax.ShapeDtypeStruct((RMAX, kv), f32),
        ),
        in_specs=[vmem, pl.BlockSpec(memory_space=pl.ANY)] + [vmem] * 6,
        out_specs=(vmem, vmem, vmem),
        scratch_shapes=[
            pltpu.VMEM((n, rows, kv + n * cap), bf16),
            pltpu.VMEM((n, cap, width), bf16),
            pltpu.VMEM((n, cols, RMAX), bf16),
            pltpu.VMEM((n, n * cap, RMAX), bf16),
            pltpu.VMEM((n, cap, kv), bf16),
            pltpu.VMEM((n, n, cap, cols), bf16),
            pltpu.VMEM((n, rows, cols), bf16),
            dma((n,)),
            dma((n,)),
            dma((n,)),
            dma((n,)),
            dma((n,)),
            dma((n,)),
            dma((groups, n)),
            dma((groups, n)),
            dma((n,)),
            dma((n,)),
            dma((n,)),
            dma((n,)),
            dma,
        ],
        compiler_params=pltpu.CompilerParams(
            collective_id=0, has_side_effects=True, vmem_limit_bytes=56 * 1024 * 1024
        ),
    )(
        pack,
        sent,
        adapter_down[0],
        adapter_up[0],
        base_weight,
        mask,
        jnp.broadcast_to(my_scale, (1, RMAX)),
        jnp.broadcast_to(scales[:, None, None], (tenants, 1, cols)),
    )
    return out, grad_down[None], grad_up[None]


def on_device(
    activations,
    grad_out,
    base_weight,
    adapter_down,
    adapter_up,
    row_tenant,
    rank_bucket,
    owner_slot,
):
    bf16 = jnp.bfloat16
    rows, width = activations.shape
    kv = grad_out.shape[1]
    tenants = rank_bucket.shape[0]
    n = lax.axis_size("fsdp")
    groups = lax.axis_size("groups")
    me = lax.axis_index("fsdp")
    my_group = lax.axis_index("groups")
    cap = max(2, 2 * rows // tenants)
    cols = width // n
    part = cols // groups
    down, up = adapter_down[0], adapter_up[0]

    my_part = lax.dynamic_index_in_dim(
        down.reshape(n, groups, part, RMAX), my_group, axis=1, keepdims=False
    )
    parts = lax.all_to_all(my_part, "fsdp", split_axis=0, concat_axis=0, tiled=True)
    slices = lax.all_gather(parts, "groups", axis=1, tiled=True)

    grad_all = lax.all_gather(grad_out, "fsdp", axis=0, tiled=True).reshape(n, rows, kv)
    tenant = lax.all_gather(row_tenant[:, 0], "fsdp", axis=0, tiled=True).reshape(n, rows)

    same = tenant[:, :, None] == tenant[:, None, :]
    before = jnp.arange(rows)[None, :, None] > jnp.arange(rows)[None, None, :]
    within = jnp.sum((same & before).astype(jnp.int32), axis=2)
    hot = tenant[:, :, None] == jnp.arange(tenants, dtype=jnp.int32)
    slot = jnp.sum(jnp.where(hot, owner_slot, 0), axis=2)
    place = slot * cap + within
    perm = (
        place[:, None, :] == jnp.arange(tenants * cap, dtype=jnp.int32)[None, :, None]
    ).astype(bf16)
    perm_mine = lax.dynamic_index_in_dim(perm, me, axis=0, keepdims=False)
    pick = lax.dynamic_slice_in_dim(perm, me * cap, cap, axis=1)

    bucket_of_slot = jnp.sum(
        jnp.where(owner_slot[None, :] == jnp.arange(tenants)[:, None], rank_bucket[None, :], 0),
        axis=1,
    )
    ranks = jnp.where(bucket_of_slot == 0, R_SMALL, jnp.where(bucket_of_slot == 1, R_MID, RMAX))
    scales = ALPHA / ranks.astype(jnp.float32)
    my_rank, my_scale = ranks[me], scales[me]
    mask = (jnp.arange(RMAX, dtype=jnp.int32) < my_rank).astype(jnp.float32)

    sent = dot(perm_mine, activations, ((1,), (0,))).astype(bf16)
    came = lax.all_to_all(
        sent.reshape(n, cap, width), "fsdp", split_axis=0, concat_axis=0, tiled=True
    ).reshape(n * cap, width)

    grads = dot(pick, grad_all, ((2,), (1,)), ((0,), (0,))).astype(bf16).reshape(n * cap, kv)
    back = (dot(grads, up, ((1,), (1,))) * mask).astype(bf16)
    backs = lax.all_gather(back, "fsdp", axis=0, tiled=True).reshape(tenants, n * cap, RMAX)

    lora = dot(backs, slices, ((2,), (2,)), ((0,), (0,))) * scales[:, None, None]
    lora = lora.astype(bf16).reshape(tenants, n, cap, cols)
    lora = jnp.transpose(lora, (1, 0, 2, 3)).reshape(n, tenants * cap, cols)
    lora = dot(perm, lora, ((1,), (1,)), ((0,), (0,)))
    base = dot(grad_all.reshape(n * rows, kv), base_weight, ((1,), (1,))).astype(bf16)
    total = (base.reshape(n, rows, cols).astype(jnp.float32) + lora).astype(bf16)
    input_gradient = lax.all_to_all(
        total.reshape(n * rows, cols), "fsdp", split_axis=0, concat_axis=1, tiled=True
    )

    hidden = (dot(came, down, ((1,), (0,))) * mask).astype(bf16)
    grad_down = my_scale * dot(came, back, ((0,), (0,)))
    grad_up = my_scale * dot(hidden, grads, ((0,), (0,)))
    return input_gradient, grad_down[None], grad_up[None]


def solution(mesh):
    rows = P(("groups", "fsdp"), None)
    devices = mesh.shape["groups"] * mesh.shape["fsdp"]

    def call(*args):
        tokens = args[0].shape[0] // devices
        tenants = args[6].shape[0]
        cap = 2 * tokens // tenants
        fits = cap % 16 == 0 and mesh.shape["fsdp"] % 4 == 0 and tenants == mesh.shape["fsdp"]
        return mapped(one_kernel if fits else on_device)(*args)

    mapped = lambda body: jax.shard_map(
        body,
        mesh=mesh,
        in_specs=(
            rows,
            rows,
            P("fsdp", None),
            P("fsdp", None, None),
            P("fsdp", None, None),
            rows,
            P(),
            P(),
        ),
        out_specs=(
            rows,
            P(("groups", "fsdp"), None, None),
            P(("groups", "fsdp"), None, None),
        ),
        check_vma=False,
    )
    return call
```

```python
import functools

import jax
import jax.numpy as jnp
from jax import lax
from jax.experimental import pallas as pl
from jax.experimental.pallas import tpu as pltpu
from jax.sharding import PartitionSpec as P

R_SMALL = 8
R_MID = 32
RMAX = 128
ALPHA = 16.0


def dot(a, b, dims, batch=((), ())):
    return lax.dot_general(a, b, (dims, batch), preferred_element_type=jnp.float32)


MESH = pl.DeviceIdType.MESH
PIECES = 4


def exchange_kernel(
    n,
    groups,
    pack_ref,
    rows_ref,
    down_ref,
    up_ref,
    weight_ref,
    mask_ref,
    my_scale_ref,
    scales_ref,
    out_ref,
    grad_down_ref,
    grad_up_ref,
    packs,
    came,
    slices,
    backs,
    grads,
    lora,
    total,
    sent_ref,
    pack_send,
    pack_recv,
    back_send,
    back_recv,
    down_send,
    down_recv,
    x_send,
    x_recv,
    act_send,
    act_recv,
    out_send,
    out_recv,
):
    bf16 = jnp.bfloat16
    me = lax.axis_index("fsdp")
    group = lax.axis_index("groups")
    cap, width = sent_ref.shape[1], sent_ref.shape[2]
    rows = pack_ref.shape[0]
    kv = grads.shape[2]
    cols = slices.shape[1]
    part = cols // groups
    w = me % 4
    across = me - w + (w + 2) % 4
    beside = me + 1 - 2 * (w % 2)
    line = n // 4

    def remote(src, dst, send, recv, to, to_group=None):
        return pltpu.make_async_remote_copy(
            src_ref=src,
            dst_ref=dst,
            send_sem=send,
            recv_sem=recv,
            device_id=(group if to_group is None else to_group, to),
            device_id_type=MESH,
        )

    def peer(k):
        return lax.rem(me + k, n)

    def source(k):
        return lax.rem(me + n - k, n)

    def loop(first, last, body):
        lax.fori_loop(first, last, lambda k, c: (body(k), c)[1], 0)

    barrier = pltpu.get_barrier_semaphore()
    loop(1, n, lambda k: pl.semaphore_signal(
        barrier, inc=1, device_id=(group, peer(k)), device_id_type=MESH))
    for d in range(1, groups):
        pl.semaphore_signal(
            barrier, inc=1, device_id=((group + d) % groups, me), device_id_type=MESH)

    packs[me] = pack_ref[...]
    slices[me] = down_ref[pl.ds(pl.multiple_of(me * cols, cols), cols), :]
    pl.semaphore_wait(barrier, n - 1 + groups - 1)

    def hop(buf, send, recv, pieces, i, number, p, to):
        size = buf.shape[1] // pieces
        spot = buf.at[i, pl.ds(p * size, size), :]
        return remote(spot, spot, send.at[p, number], recv.at[p, number], to)

    def gather_start(buf, send, recv, pieces):
        for p in range(pieces):
            for k in range(1, line):
                hop(buf, send, recv, pieces, me, k, p, peer(4 * k)).start()
            hop(buf, send, recv, pieces, me, line, p, across).start()
            hop(buf, send, recv, pieces, me, 2 * line, p, beside).start()

    def gather_finish(buf, send, recv, pieces):
        def copy(i, number, p, to):
            return hop(buf, send, recv, pieces, i, number, p, to)

        def from_line(origin, k):
            return lax.rem(origin + n - 4 * k, n)

        other = beside - beside % 4 + (beside % 4 + 2) % 4
        for p in range(pieces):
            for k in range(1, line):
                i = source(4 * k)
                copy(i, k, p, peer(4 * k)).wait_recv()
                copy(i, line + k, p, across).start()
                copy(i, 2 * line + k, p, beside).start()
        for p in range(pieces):
            for k in range(line):
                i = from_line(across, k)
                copy(i, line + k, p, across).wait_recv()
                copy(i, 3 * line + k, p, beside).start()
        for p in range(pieces):
            for k in range(line):
                copy(from_line(beside, k), 2 * line + k, p, beside).wait_recv()
            for k in range(line):
                copy(from_line(other, k), 3 * line + k, p, beside).wait_recv()

    def gather_sent(buf, send, recv, pieces):
        for p in range(pieces):
            for k in range(1, 4 * line):
                hop(buf, send, recv, pieces, me, k, p, beside).wait_send()

    def down_part(k):
        j = peer(k)
        start = pl.multiple_of(j * cols + group * part, part)
        return remote(
            down_ref.at[pl.ds(start, part), :],
            slices.at[me, pl.ds(pl.multiple_of(group * part, part), part), :],
            down_send.at[k], down_recv.at[k], j)

    def place_of(k, owner):
        return slices.at[source(k), pl.ds(pl.multiple_of(owner * part, part), part), :]

    gather_start(packs, pack_send, pack_recv, PIECES)
    loop(1, n, lambda k: down_part(k).start())

    def order_rows(c):
        at = pl.ds(pl.multiple_of(c * 1024, 1024), 1024)
        moved = dot(pack_ref[:, kv:], rows_ref[:, at], ((0,), (0,))).astype(bf16)
        sent_ref[:, :, at] = moved.reshape(n, cap, 1024)

    loop(0, width // 1024, order_rows)
    gather_finish(packs, pack_send, pack_recv, PIECES)

    def act(k):
        j = peer(k)
        return remote(sent_ref.at[j], came.at[me], act_send.at[k], act_recv.at[k], j)

    wanted = (
        lax.broadcasted_iota(jnp.int32, (n * cap, cap), 0)
        == lax.broadcasted_iota(jnp.int32, (n * cap, cap), 1) + me * cap
    ).astype(bf16)

    def pick(b):
        chosen = dot(packs[b, :, kv:], wanted, ((1,), (0,))).astype(bf16)
        grads[b] = dot(chosen, packs[b, :, :kv], ((0,), (0,))).astype(bf16)

    loop(0, n, pick)
    back = dot(grads[...].reshape(n * cap, kv), up_ref[...], ((1,), (1,))) * mask_ref[...]
    backs[me] = back.astype(bf16)
    gather_start(backs, back_send, back_recv, 1)

    loop(1, n, lambda k: act(k).start())

    def relay(k):
        remote(place_of(k, group), place_of(k, group), down_send.at[k], down_recv.at[k],
               peer(k)).wait_recv()
        for d in range(1, groups):
            remote(place_of(k, group), place_of(k, group), x_send.at[d, k], x_recv.at[d, k],
                   me, (group + d) % groups).start()

    loop(1, n, relay)
    gather_finish(backs, back_send, back_recv, 1)

    def base(i):
        some = pl.ds(i * 4, 4)
        block = packs[some, :, :kv].reshape(4 * rows, kv)
        product = dot(block, weight_ref[...], ((1,), (1,))).astype(bf16)
        total[some] = product.reshape(4, rows, cols)

    loop(0, line, base)

    def relayed(k):
        for d in range(1, groups):
            spot = place_of(k, (group + groups - d) % groups)
            remote(spot, spot, x_send.at[d, k], x_recv.at[d, k], me,
                   (group + d) % groups).wait_recv()

    loop(1, n, relayed)

    def low_rank(t):
        term = dot(backs[t], slices[t], ((1,), (1,))) * scales_ref[t]
        lora[:, t] = term.astype(bf16).reshape(n, cap, cols)

    loop(0, n, low_rank)

    def combine(b):
        term = dot(packs[b, :, kv:], lora[b].reshape(n * cap, cols), ((1,), (0,)))
        total[b] = (total[b].astype(jnp.float32) + term).astype(bf16)

    def columns(i):
        return out_ref.at[:, pl.ds(pl.multiple_of(i * cols, cols), cols)]

    def result(k):
        j = peer(k)
        return remote(total.at[j], columns(me), out_send.at[k], out_recv.at[k], j)

    def combine_and_send(k):
        combine(peer(k))
        result(k).start()

    loop(1, n, combine_and_send)
    combine(me)
    out_ref[:, pl.ds(pl.multiple_of(me * cols, cols), cols)] = total[me]

    def arrived(k):
        spot = came.at[source(k)]
        remote(spot, spot, act_send.at[k], act_recv.at[k], peer(k)).wait_recv()

    loop(1, n, arrived)
    came[me] = sent_ref[me]
    my_back = backs[me]
    chunk = 1024
    hidden = jnp.zeros((n * cap, RMAX), jnp.float32)
    for c in range(width // chunk):
        at = pl.ds(c * chunk, chunk)
        held = came[:, :, at].reshape(n * cap, chunk)
        hidden += dot(held, down_ref[at, :], ((1,), (0,)))
        grad_down_ref[at, :] = dot(held, my_back, ((0,), (0,))) * my_scale_ref[...]
    hidden = (hidden * mask_ref[...]).astype(bf16)
    up_scale = my_scale_ref[0:1, 0:1]
    grad_up_ref[...] = (
        dot(hidden, grads[...].reshape(n * cap, kv), ((0,), (0,))) * up_scale
    )

    def received(k):
        spot = columns(source(k))
        remote(total.at[me], spot, out_send.at[k], out_recv.at[k], peer(k)).wait_recv()

    loop(1, n, received)
    gather_sent(packs, pack_send, pack_recv, PIECES)
    gather_sent(backs, back_send, back_recv, 1)

    def all_sent(k):
        down_part(k).wait_send()
        for d in range(1, groups):
            remote(place_of(k, group), place_of(k, group), x_send.at[d, k], x_recv.at[d, k],
                   me, (group + d) % groups).wait_send()
        act(k).wait_send()
        result(k).wait_send()

    loop(1, n, all_sent)


def one_kernel(
    activations,
    grad_out,
    base_weight,
    adapter_down,
    adapter_up,
    row_tenant,
    rank_bucket,
    owner_slot,
):
    bf16, f32 = jnp.bfloat16, jnp.float32
    rows, width = activations.shape
    kv = grad_out.shape[1]
    tenants = rank_bucket.shape[0]
    n = lax.axis_size("fsdp")
    groups = lax.axis_size("groups")
    me = lax.axis_index("fsdp")
    cap = 2 * rows // tenants
    cols = width // n

    tenant = row_tenant[:, 0]
    same = tenant[:, None] == tenant[None, :]
    before = jnp.arange(rows)[:, None] > jnp.arange(rows)[None, :]
    within = jnp.sum((same & before).astype(jnp.int32), axis=1)
    hot = tenant[:, None] == jnp.arange(tenants, dtype=jnp.int32)
    place = jnp.sum(jnp.where(hot, owner_slot, 0), axis=1) * cap + within
    perm = (place[:, None] == jnp.arange(n * cap, dtype=jnp.int32)[None, :]).astype(bf16)
    bucket_of_slot = jnp.sum(
        jnp.where(owner_slot[None, :] == jnp.arange(tenants)[:, None], rank_bucket[None, :], 0),
        axis=1,
    )
    ranks = jnp.where(bucket_of_slot == 0, R_SMALL, jnp.where(bucket_of_slot == 1, R_MID, RMAX))
    scales = ALPHA / ranks.astype(f32)
    mine = jnp.arange(tenants, dtype=jnp.int32) == me
    my_rank = jnp.sum(jnp.where(mine, ranks, 0))
    my_scale = jnp.sum(jnp.where(mine, scales, 0.0))
    mask = (jnp.arange(RMAX, dtype=jnp.int32) < my_rank).astype(f32)[None, :]
    pack = jnp.concatenate([grad_out, perm], axis=1)

    vmem = pl.BlockSpec(memory_space=pltpu.VMEM)
    dma = pltpu.SemaphoreType.DMA
    out, grad_down, grad_up = pl.pallas_call(
        functools.partial(exchange_kernel, n, groups),
        out_shape=(
            jax.ShapeDtypeStruct((rows, width), bf16),
            jax.ShapeDtypeStruct((width, RMAX), f32),
            jax.ShapeDtypeStruct((RMAX, kv), f32),
        ),
        in_specs=[vmem] * 8,
        out_specs=(vmem, vmem, vmem),
        scratch_shapes=[
            pltpu.VMEM((n, rows, kv + n * cap), bf16),
            pltpu.VMEM((n, cap, width), bf16),
            pltpu.VMEM((n, cols, RMAX), bf16),
            pltpu.VMEM((n, n * cap, RMAX), bf16),
            pltpu.VMEM((n, cap, kv), bf16),
            pltpu.VMEM((n, n, cap, cols), bf16),
            pltpu.VMEM((n, rows, cols), bf16),
            pltpu.VMEM((n, cap, width), bf16),
            dma((PIECES, n)),
            dma((PIECES, n)),
            dma((1, n)),
            dma((1, n)),
            dma((n,)),
            dma((n,)),
            dma((groups, n)),
            dma((groups, n)),
            dma((n,)),
            dma((n,)),
            dma((n,)),
            dma((n,)),
        ],
        compiler_params=pltpu.CompilerParams(
            collective_id=0, has_side_effects=True, vmem_limit_bytes=56 * 1024 * 1024
        ),
    )(
        pack,
        activations,
        adapter_down[0],
        adapter_up[0],
        base_weight,
        mask,
        jnp.broadcast_to(my_scale, (1, RMAX)),
        jnp.broadcast_to(scales[:, None, None], (tenants, 1, cols)),
    )
    return out, grad_down[None], grad_up[None]


def on_device(
    activations,
    grad_out,
    base_weight,
    adapter_down,
    adapter_up,
    row_tenant,
    rank_bucket,
    owner_slot,
):
    bf16 = jnp.bfloat16
    rows, width = activations.shape
    kv = grad_out.shape[1]
    tenants = rank_bucket.shape[0]
    n = lax.axis_size("fsdp")
    groups = lax.axis_size("groups")
    me = lax.axis_index("fsdp")
    my_group = lax.axis_index("groups")
    cap = max(2, 2 * rows // tenants)
    cols = width // n
    part = cols // groups
    down, up = adapter_down[0], adapter_up[0]

    my_part = lax.dynamic_index_in_dim(
        down.reshape(n, groups, part, RMAX), my_group, axis=1, keepdims=False
    )
    parts = lax.all_to_all(my_part, "fsdp", split_axis=0, concat_axis=0, tiled=True)
    slices = lax.all_gather(parts, "groups", axis=1, tiled=True)

    grad_all = lax.all_gather(grad_out, "fsdp", axis=0, tiled=True).reshape(n, rows, kv)
    tenant = lax.all_gather(row_tenant[:, 0], "fsdp", axis=0, tiled=True).reshape(n, rows)

    same = tenant[:, :, None] == tenant[:, None, :]
    before = jnp.arange(rows)[None, :, None] > jnp.arange(rows)[None, None, :]
    within = jnp.sum((same & before).astype(jnp.int32), axis=2)
    hot = tenant[:, :, None] == jnp.arange(tenants, dtype=jnp.int32)
    slot = jnp.sum(jnp.where(hot, owner_slot, 0), axis=2)
    place = slot * cap + within
    perm = (
        place[:, None, :] == jnp.arange(tenants * cap, dtype=jnp.int32)[None, :, None]
    ).astype(bf16)
    perm_mine = lax.dynamic_index_in_dim(perm, me, axis=0, keepdims=False)
    pick = lax.dynamic_slice_in_dim(perm, me * cap, cap, axis=1)

    bucket_of_slot = jnp.sum(
        jnp.where(owner_slot[None, :] == jnp.arange(tenants)[:, None], rank_bucket[None, :], 0),
        axis=1,
    )
    ranks = jnp.where(bucket_of_slot == 0, R_SMALL, jnp.where(bucket_of_slot == 1, R_MID, RMAX))
    scales = ALPHA / ranks.astype(jnp.float32)
    my_rank, my_scale = ranks[me], scales[me]
    mask = (jnp.arange(RMAX, dtype=jnp.int32) < my_rank).astype(jnp.float32)

    sent = dot(perm_mine, activations, ((1,), (0,))).astype(bf16)
    came = lax.all_to_all(
        sent.reshape(n, cap, width), "fsdp", split_axis=0, concat_axis=0, tiled=True
    ).reshape(n * cap, width)

    grads = dot(pick, grad_all, ((2,), (1,)), ((0,), (0,))).astype(bf16).reshape(n * cap, kv)
    back = (dot(grads, up, ((1,), (1,))) * mask).astype(bf16)
    backs = lax.all_gather(back, "fsdp", axis=0, tiled=True).reshape(tenants, n * cap, RMAX)

    lora = dot(backs, slices, ((2,), (2,)), ((0,), (0,))) * scales[:, None, None]
    lora = lora.astype(bf16).reshape(tenants, n, cap, cols)
    lora = jnp.transpose(lora, (1, 0, 2, 3)).reshape(n, tenants * cap, cols)
    lora = dot(perm, lora, ((1,), (1,)), ((0,), (0,)))
    base = dot(grad_all.reshape(n * rows, kv), base_weight, ((1,), (1,))).astype(bf16)
    total = (base.reshape(n, rows, cols).astype(jnp.float32) + lora).astype(bf16)
    input_gradient = lax.all_to_all(
        total.reshape(n * rows, cols), "fsdp", split_axis=0, concat_axis=1, tiled=True
    )

    hidden = (dot(came, down, ((1,), (0,))) * mask).astype(bf16)
    grad_down = my_scale * dot(came, back, ((0,), (0,)))
    grad_up = my_scale * dot(hidden, grads, ((0,), (0,)))
    return input_gradient, grad_down[None], grad_up[None]


def solution(mesh):
    rows = P(("groups", "fsdp"), None)
    devices = mesh.shape["groups"] * mesh.shape["fsdp"]

    def call(*args):
        tokens = args[0].shape[0] // devices
        tenants = args[6].shape[0]
        cap = 2 * tokens // tenants
        fits = cap % 16 == 0 and mesh.shape["fsdp"] % 4 == 0 and tenants == mesh.shape["fsdp"]
        return mapped(one_kernel if fits else on_device)(*args)

    mapped = lambda body: jax.shard_map(
        body,
        mesh=mesh,
        in_specs=(
            rows,
            rows,
            P("fsdp", None),
            P("fsdp", None, None),
            P("fsdp", None, None),
            rows,
            P(),
            P(),
        ),
        out_specs=(
            rows,
            P(("groups", "fsdp"), None, None),
            P(("groups", "fsdp"), None, None),
        ),
        check_vma=False,
    )
    return call
```

```python
import functools

import jax
import jax.numpy as jnp
from jax import lax
from jax.experimental import pallas as pl
from jax.experimental.pallas import tpu as pltpu
from jax.sharding import PartitionSpec as P

R_SMALL = 8
R_MID = 32
RMAX = 128
ALPHA = 16.0


def dot(a, b, dims, batch=((), ())):
    return lax.dot_general(a, b, (dims, batch), preferred_element_type=jnp.float32)


MESH = pl.DeviceIdType.MESH
PIECES = 4


def exchange_kernel(
    n,
    groups,
    pack_ref,
    rows_ref,
    down_ref,
    up_ref,
    weight_ref,
    mask_ref,
    my_scale_ref,
    scales_ref,
    out_ref,
    grad_down_ref,
    grad_up_ref,
    packs,
    came,
    slices,
    backs,
    grads,
    lora,
    total,
    sent_ref,
    pack_send,
    pack_recv,
    back_send,
    back_recv,
    down_send,
    down_recv,
    x_send,
    x_recv,
    act_send,
    act_recv,
    out_send,
    out_recv,
):
    bf16 = jnp.bfloat16
    me = lax.axis_index("fsdp")
    group = lax.axis_index("groups")
    cap, width = sent_ref.shape[1], sent_ref.shape[2]
    rows = pack_ref.shape[0]
    kv = grads.shape[2]
    cols = slices.shape[1]
    part = cols // groups
    w = me % 4
    across = me - w + (w + 2) % 4
    beside = me + 1 - 2 * (w % 2)
    line = n // 4

    def remote(src, dst, send, recv, to, to_group=None):
        return pltpu.make_async_remote_copy(
            src_ref=src,
            dst_ref=dst,
            send_sem=send,
            recv_sem=recv,
            device_id=(group if to_group is None else to_group, to),
            device_id_type=MESH,
        )

    def peer(k):
        return lax.rem(me + k, n)

    def source(k):
        return lax.rem(me + n - k, n)

    def loop(first, last, body):
        lax.fori_loop(first, last, lambda k, c: (body(k), c)[1], 0)

    barrier = pltpu.get_barrier_semaphore()
    loop(1, n, lambda k: pl.semaphore_signal(
        barrier, inc=1, device_id=(group, peer(k)), device_id_type=MESH))
    for d in range(1, groups):
        pl.semaphore_signal(
            barrier, inc=1, device_id=((group + d) % groups, me), device_id_type=MESH)

    packs[me] = pack_ref[...]
    slices[me] = down_ref[pl.ds(pl.multiple_of(me * cols, cols), cols), :]
    pl.semaphore_wait(barrier, n - 1 + groups - 1)

    def hop(buf, send, recv, pieces, i, number, p, to):
        size = buf.shape[1] // pieces
        spot = buf.at[i, pl.ds(p * size, size), :]
        return remote(spot, spot, send.at[p, number], recv.at[p, number], to)

    def gather_start(buf, send, recv, pieces):
        for p in range(pieces):
            for k in range(1, line):
                hop(buf, send, recv, pieces, me, k, p, peer(4 * k)).start()
            hop(buf, send, recv, pieces, me, line, p, across).start()
            hop(buf, send, recv, pieces, me, 2 * line, p, beside).start()

    def gather_finish(buf, send, recv, pieces):
        def copy(i, number, p, to):
            return hop(buf, send, recv, pieces, i, number, p, to)

        def from_line(origin, k):
            return lax.rem(origin + n - 4 * k, n)

        other = beside - beside % 4 + (beside % 4 + 2) % 4
        for p in range(pieces):
            for k in range(1, line):
                i = source(4 * k)
                copy(i, k, p, peer(4 * k)).wait_recv()
                copy(i, line + k, p, across).start()
                copy(i, 2 * line + k, p, beside).start()
        for p in range(pieces):
            for k in range(line):
                i = from_line(across, k)
                copy(i, line + k, p, across).wait_recv()
                copy(i, 3 * line + k, p, beside).start()
        for p in range(pieces):
            for k in range(line):
                copy(from_line(beside, k), 2 * line + k, p, beside).wait_recv()
            for k in range(line):
                copy(from_line(other, k), 3 * line + k, p, beside).wait_recv()

    def gather_sent(buf, send, recv, pieces):
        for p in range(pieces):
            for k in range(1, 4 * line):
                hop(buf, send, recv, pieces, me, k, p, beside).wait_send()

    def down_part(k):
        j = peer(k)
        start = pl.multiple_of(j * cols + group * part, part)
        return remote(
            down_ref.at[pl.ds(start, part), :],
            slices.at[me, pl.ds(pl.multiple_of(group * part, part), part), :],
            down_send.at[k], down_recv.at[k], j)

    def place_of(k, owner):
        return slices.at[source(k), pl.ds(pl.multiple_of(owner * part, part), part), :]

    gather_start(packs, pack_send, pack_recv, PIECES)
    loop(1, n, lambda k: down_part(k).start())

    def order_rows(c):
        at = pl.ds(pl.multiple_of(c * 1024, 1024), 1024)
        moved = dot(pack_ref[:, kv:], rows_ref[:, at], ((0,), (0,))).astype(bf16)
        sent_ref[:, :, at] = moved.reshape(n, cap, 1024)

    loop(0, width // 1024, order_rows)
    gather_finish(packs, pack_send, pack_recv, PIECES)

    def act(k):
        j = peer(k)
        return remote(sent_ref.at[j], came.at[me], act_send.at[k], act_recv.at[k], j)

    def relay(k):
        remote(place_of(k, group), place_of(k, group), down_send.at[k], down_recv.at[k],
               peer(k)).wait_recv()
        for d in range(1, groups):
            remote(place_of(k, group), place_of(k, group), x_send.at[d, k], x_recv.at[d, k],
                   me, (group + d) % groups).start()

    loop(1, n, relay)

    wanted = (
        lax.broadcasted_iota(jnp.int32, (n * cap, cap), 0)
        == lax.broadcasted_iota(jnp.int32, (n * cap, cap), 1) + me * cap
    ).astype(bf16)

    def pick(b):
        chosen = dot(packs[b, :, kv:], wanted, ((1,), (0,))).astype(bf16)
        grads[b] = dot(chosen, packs[b, :, :kv], ((0,), (0,))).astype(bf16)

    loop(0, n, pick)
    back = dot(grads[...].reshape(n * cap, kv), up_ref[...], ((1,), (1,))) * mask_ref[...]
    backs[me] = back.astype(bf16)
    gather_start(backs, back_send, back_recv, 1)

    loop(1, n, lambda k: act(k).start())

    gather_finish(backs, back_send, back_recv, 1)

    def base(i):
        some = pl.ds(i * 4, 4)
        block = packs[some, :, :kv].reshape(4 * rows, kv)
        product = dot(block, weight_ref[...], ((1,), (1,))).astype(bf16)
        total[some] = product.reshape(4, rows, cols)

    loop(0, line, base)

    def relayed(k):
        for d in range(1, groups):
            spot = place_of(k, (group + groups - d) % groups)
            remote(spot, spot, x_send.at[d, k], x_recv.at[d, k], me,
                   (group + d) % groups).wait_recv()

    loop(1, n, relayed)

    def low_rank(t):
        term = dot(backs[t], slices[t], ((1,), (1,))) * scales_ref[t]
        lora[:, t] = term.astype(bf16).reshape(n, cap, cols)

    loop(0, n, low_rank)

    def combine(b):
        term = dot(packs[b, :, kv:], lora[b].reshape(n * cap, cols), ((1,), (0,)))
        total[b] = (total[b].astype(jnp.float32) + term).astype(bf16)

    def columns(i):
        return out_ref.at[:, pl.ds(pl.multiple_of(i * cols, cols), cols)]

    def result(k):
        j = peer(k)
        return remote(total.at[j], columns(me), out_send.at[k], out_recv.at[k], j)

    def combine_and_send(k):
        combine(peer(k))
        result(k).start()

    loop(1, n, combine_and_send)
    combine(me)
    out_ref[:, pl.ds(pl.multiple_of(me * cols, cols), cols)] = total[me]

    def arrived(k):
        spot = came.at[source(k)]
        remote(spot, spot, act_send.at[k], act_recv.at[k], peer(k)).wait_recv()

    loop(1, n, arrived)
    came[me] = sent_ref[me]
    my_back = backs[me]
    chunk = 1024
    hidden = jnp.zeros((n * cap, RMAX), jnp.float32)
    for c in range(width // chunk):
        at = pl.ds(c * chunk, chunk)
        held = came[:, :, at].reshape(n * cap, chunk)
        hidden += dot(held, down_ref[at, :], ((1,), (0,)))
        grad_down_ref[at, :] = dot(held, my_back, ((0,), (0,))) * my_scale_ref[...]
    hidden = (hidden * mask_ref[...]).astype(bf16)
    up_scale = my_scale_ref[0:1, 0:1]
    grad_up_ref[...] = (
        dot(hidden, grads[...].reshape(n * cap, kv), ((0,), (0,))) * up_scale
    )

    def received(k):
        spot = columns(source(k))
        remote(total.at[me], spot, out_send.at[k], out_recv.at[k], peer(k)).wait_recv()

    loop(1, n, received)
    gather_sent(packs, pack_send, pack_recv, PIECES)
    gather_sent(backs, back_send, back_recv, 1)

    def all_sent(k):
        down_part(k).wait_send()
        for d in range(1, groups):
            remote(place_of(k, group), place_of(k, group), x_send.at[d, k], x_recv.at[d, k],
                   me, (group + d) % groups).wait_send()
        act(k).wait_send()
        result(k).wait_send()

    loop(1, n, all_sent)


def one_kernel(
    activations,
    grad_out,
    base_weight,
    adapter_down,
    adapter_up,
    row_tenant,
    rank_bucket,
    owner_slot,
):
    bf16, f32 = jnp.bfloat16, jnp.float32
    rows, width = activations.shape
    kv = grad_out.shape[1]
    tenants = rank_bucket.shape[0]
    n = lax.axis_size("fsdp")
    groups = lax.axis_size("groups")
    me = lax.axis_index("fsdp")
    cap = 2 * rows // tenants
    cols = width // n

    tenant = row_tenant[:, 0]
    same = tenant[:, None] == tenant[None, :]
    before = jnp.arange(rows)[:, None] > jnp.arange(rows)[None, :]
    within = jnp.sum((same & before).astype(jnp.int32), axis=1)
    hot = tenant[:, None] == jnp.arange(tenants, dtype=jnp.int32)
    place = jnp.sum(jnp.where(hot, owner_slot, 0), axis=1) * cap + within
    perm = (place[:, None] == jnp.arange(n * cap, dtype=jnp.int32)[None, :]).astype(bf16)
    bucket_of_slot = jnp.sum(
        jnp.where(owner_slot[None, :] == jnp.arange(tenants)[:, None], rank_bucket[None, :], 0),
        axis=1,
    )
    ranks = jnp.where(bucket_of_slot == 0, R_SMALL, jnp.where(bucket_of_slot == 1, R_MID, RMAX))
    scales = ALPHA / ranks.astype(f32)
    mine = jnp.arange(tenants, dtype=jnp.int32) == me
    my_rank = jnp.sum(jnp.where(mine, ranks, 0))
    my_scale = jnp.sum(jnp.where(mine, scales, 0.0))
    mask = (jnp.arange(RMAX, dtype=jnp.int32) < my_rank).astype(f32)[None, :]
    pack = jnp.concatenate([grad_out, perm], axis=1)

    vmem = pl.BlockSpec(memory_space=pltpu.VMEM)
    dma = pltpu.SemaphoreType.DMA
    out, grad_down, grad_up = pl.pallas_call(
        functools.partial(exchange_kernel, n, groups),
        out_shape=(
            jax.ShapeDtypeStruct((rows, width), bf16),
            jax.ShapeDtypeStruct((width, RMAX), f32),
            jax.ShapeDtypeStruct((RMAX, kv), f32),
        ),
        in_specs=[vmem] * 8,
        out_specs=(vmem, vmem, vmem),
        scratch_shapes=[
            pltpu.VMEM((n, rows, kv + n * cap), bf16),
            pltpu.VMEM((n, cap, width), bf16),
            pltpu.VMEM((n, cols, RMAX), bf16),
            pltpu.VMEM((n, n * cap, RMAX), bf16),
            pltpu.VMEM((n, cap, kv), bf16),
            pltpu.VMEM((n, n, cap, cols), bf16),
            pltpu.VMEM((n, rows, cols), bf16),
            pltpu.VMEM((n, cap, width), bf16),
            dma((PIECES, n)),
            dma((PIECES, n)),
            dma((1, n)),
            dma((1, n)),
            dma((n,)),
            dma((n,)),
            dma((groups, n)),
            dma((groups, n)),
            dma((n,)),
            dma((n,)),
            dma((n,)),
            dma((n,)),
        ],
        compiler_params=pltpu.CompilerParams(
            collective_id=0, has_side_effects=True, vmem_limit_bytes=56 * 1024 * 1024
        ),
    )(
        pack,
        activations,
        adapter_down[0],
        adapter_up[0],
        base_weight,
        mask,
        jnp.broadcast_to(my_scale, (1, RMAX)),
        jnp.broadcast_to(scales[:, None, None], (tenants, 1, cols)),
    )
    return out, grad_down[None], grad_up[None]


def on_device(
    activations,
    grad_out,
    base_weight,
    adapter_down,
    adapter_up,
    row_tenant,
    rank_bucket,
    owner_slot,
):
    bf16 = jnp.bfloat16
    rows, width = activations.shape
    kv = grad_out.shape[1]
    tenants = rank_bucket.shape[0]
    n = lax.axis_size("fsdp")
    groups = lax.axis_size("groups")
    me = lax.axis_index("fsdp")
    my_group = lax.axis_index("groups")
    cap = max(2, 2 * rows // tenants)
    cols = width // n
    part = cols // groups
    down, up = adapter_down[0], adapter_up[0]

    my_part = lax.dynamic_index_in_dim(
        down.reshape(n, groups, part, RMAX), my_group, axis=1, keepdims=False
    )
    parts = lax.all_to_all(my_part, "fsdp", split_axis=0, concat_axis=0, tiled=True)
    slices = lax.all_gather(parts, "groups", axis=1, tiled=True)

    grad_all = lax.all_gather(grad_out, "fsdp", axis=0, tiled=True).reshape(n, rows, kv)
    tenant = lax.all_gather(row_tenant[:, 0], "fsdp", axis=0, tiled=True).reshape(n, rows)

    same = tenant[:, :, None] == tenant[:, None, :]
    before = jnp.arange(rows)[None, :, None] > jnp.arange(rows)[None, None, :]
    within = jnp.sum((same & before).astype(jnp.int32), axis=2)
    hot = tenant[:, :, None] == jnp.arange(tenants, dtype=jnp.int32)
    slot = jnp.sum(jnp.where(hot, owner_slot, 0), axis=2)
    place = slot * cap + within
    perm = (
        place[:, None, :] == jnp.arange(tenants * cap, dtype=jnp.int32)[None, :, None]
    ).astype(bf16)
    perm_mine = lax.dynamic_index_in_dim(perm, me, axis=0, keepdims=False)
    pick = lax.dynamic_slice_in_dim(perm, me * cap, cap, axis=1)

    bucket_of_slot = jnp.sum(
        jnp.where(owner_slot[None, :] == jnp.arange(tenants)[:, None], rank_bucket[None, :], 0),
        axis=1,
    )
    ranks = jnp.where(bucket_of_slot == 0, R_SMALL, jnp.where(bucket_of_slot == 1, R_MID, RMAX))
    scales = ALPHA / ranks.astype(jnp.float32)
    my_rank, my_scale = ranks[me], scales[me]
    mask = (jnp.arange(RMAX, dtype=jnp.int32) < my_rank).astype(jnp.float32)

    sent = dot(perm_mine, activations, ((1,), (0,))).astype(bf16)
    came = lax.all_to_all(
        sent.reshape(n, cap, width), "fsdp", split_axis=0, concat_axis=0, tiled=True
    ).reshape(n * cap, width)

    grads = dot(pick, grad_all, ((2,), (1,)), ((0,), (0,))).astype(bf16).reshape(n * cap, kv)
    back = (dot(grads, up, ((1,), (1,))) * mask).astype(bf16)
    backs = lax.all_gather(back, "fsdp", axis=0, tiled=True).reshape(tenants, n * cap, RMAX)

    lora = dot(backs, slices, ((2,), (2,)), ((0,), (0,))) * scales[:, None, None]
    lora = lora.astype(bf16).reshape(tenants, n, cap, cols)
    lora = jnp.transpose(lora, (1, 0, 2, 3)).reshape(n, tenants * cap, cols)
    lora = dot(perm, lora, ((1,), (1,)), ((0,), (0,)))
    base = dot(grad_all.reshape(n * rows, kv), base_weight, ((1,), (1,))).astype(bf16)
    total = (base.reshape(n, rows, cols).astype(jnp.float32) + lora).astype(bf16)
    input_gradient = lax.all_to_all(
        total.reshape(n * rows, cols), "fsdp", split_axis=0, concat_axis=1, tiled=True
    )

    hidden = (dot(came, down, ((1,), (0,))) * mask).astype(bf16)
    grad_down = my_scale * dot(came, back, ((0,), (0,)))
    grad_up = my_scale * dot(hidden, grads, ((0,), (0,)))
    return input_gradient, grad_down[None], grad_up[None]


def solution(mesh):
    rows = P(("groups", "fsdp"), None)
    devices = mesh.shape["groups"] * mesh.shape["fsdp"]

    def call(*args):
        tokens = args[0].shape[0] // devices
        tenants = args[6].shape[0]
        cap = 2 * tokens // tenants
        fits = cap % 16 == 0 and mesh.shape["fsdp"] % 4 == 0 and tenants == mesh.shape["fsdp"]
        return mapped(one_kernel if fits else on_device)(*args)

    mapped = lambda body: jax.shard_map(
        body,
        mesh=mesh,
        in_specs=(
            rows,
            rows,
            P("fsdp", None),
            P("fsdp", None, None),
            P("fsdp", None, None),
            rows,
            P(),
            P(),
        ),
        out_specs=(
            rows,
            P(("groups", "fsdp"), None, None),
            P(("groups", "fsdp"), None, None),
        ),
        check_vma=False,
    )
    return call
```
